32 devices in a mesh: groups: 2 (over x), dp: 8 (over z, y), narrow: 2 (over core).
Axes of the slice: x: 2, y: 2, z: 4, core: 2. Of those that a mesh axis runs over, the one named last changes fastest.
Arguments:
- tokens: bfloat16 [12288, 8192], P(('groups', 'dp'), 'narrow'), parts along dimension 0, may hold values from -6 to 6
- req_adapter: int32 [96], P(('groups', 'dp')), parts along dimension 0, may hold values from 0 to 15
- value_weight: bfloat16 [8192, 1024], P('narrow'), may hold values from -0.0625 to 0.0625
- adapter_down: bfloat16 [16, 64, 8192], P(None, 'dp', 'narrow'), may hold values from -0.0625 to 0.0625
- adapter_up: bfloat16 [16, 64, 1024], P(None, 'dp', 'narrow'), may hold values from -0.75 to 0.75
Outputs:
- values_out: bfloat16 [12288, 1024], P(('groups', 'dp'), 'narrow'), parts along dimension 0
The draws below stay inside these ranges and needn't reach their ends.
There are 2 independent parts, one for each index of `groups`. The reference program is written for one: setup_inputs(seed, part) draws one part's arguments, and reference() takes and returns one part's arrays. A program takes and returns all parts, laid end to end along the dimension named above; an argument that names none is the same for every part. Nothing has to cross between parts.
All inputs are finite; a program needn't handle non-finite values.
Results may differ from the reference program's by a relative error of at most 0.0053.
Values may be sent and summed in bfloat16 or wider, within the bound.
A program may use at most 128 MiB of HBM per device.

```python
import math
import jax
import jax.numpy as jnp
import numpy as np
from jax import lax

D = 8192
KVW = 1024
RANK = 64
REQ_TOK = 128
ADAPTERS = 16
TOKENS = 6144
REQUESTS = 48


def with_ends(result, stream_key, low, high):
    shape = result.shape
    place = [jax.random.randint(jax.random.fold_in(stream_key, axis), (), 0, shape[axis]) for axis in range(len(shape))]
    result = result.at[tuple(place)].set(low)
    longest = shape.index(max(shape))
    place[longest] = (place[longest] + 1) % shape[longest]
    return result.at[tuple(place)].set(high)


def shard_levels(own_key, dims, split, least, top_value):
    def one(position, blocks):
        steps = jax.random.uniform(jax.random.fold_in(jax.random.fold_in(own_key, 6), position), (blocks,), jnp.float32, least / len(split), top_value / len(split))
        return jnp.repeat(jnp.exp(steps), dims[position] // blocks).reshape((-1,) + (1,) * (len(dims) - position - 1))

    factor_of = one(*split[0])
    for cut in split[1:]:
        factor_of = factor_of * one(*cut)
    return factor_of


def cumulative_ranks(amount, lean):
    loads = [(1 << 20) // math.isqrt(standing ** lean) + 1 for standing in range(1, amount + 1)]
    scale = 1 + sum(loads) // (1 << 30)
    return np.cumsum(np.array([max(1, weight // scale) for weight in loads]))


def ranked(stream_key, shape, number_of, slope):
    listing = cumulative_ranks(number_of, slope)
    lot = jax.random.randint(jax.random.fold_in(stream_key, 1), shape, 0, int(listing[number_of - 1]))
    grade = jnp.searchsorted(jnp.asarray(listing, jnp.int32), lot, side="right")
    return jax.random.permutation(jax.random.fold_in(stream_key, 2), number_of)[grade].astype(jnp.int32)


def noise(rng, dims, spread, limit, pieces=(), dtype=jnp.bfloat16):
    values = jax.random.normal(rng, dims, jnp.float32) * spread
    if len(pieces) > 0:
        values = shard_levels(rng, dims, pieces, -0.22, 0.18) * values
    return jnp.clip(values, min=-limit, max=limit).astype(dtype)


def setup_inputs(seed: int = 0, part: int = 0) -> dict:
    key_list = jax.random.split(jax.random.key(seed), 6)
    part_keys = jax.random.split(jax.random.fold_in(key_list[5], part), 6)
    return {
        "tokens": noise(part_keys[0], (TOKENS, D), 1.0, 6.0, ((0, 8), (1, 2))),
        "req_adapter": with_ends(ranked(part_keys[1], (REQUESTS,), ADAPTERS, 2), jax.random.fold_in(part_keys[1], 3), 0, ADAPTERS - 1).astype(jnp.int32),
        "value_weight": noise(key_list[2], (D, KVW), D ** -0.5, 0.0625, ((0, 2),)),
        "adapter_down": noise(key_list[3], (ADAPTERS, RANK, D), D ** -0.5, 0.0625, ((1, 8), (2, 2))),
        "adapter_up": noise(key_list[4], (ADAPTERS, RANK, KVW), RANK ** -0.5, 0.75, ((1, 8), (2, 2))),
    }


def reference(tokens, req_adapter, value_weight, adapter_down, adapter_up):
    base = jnp.dot(tokens, value_weight, preferred_element_type=jnp.float32)
    blocks = tokens.reshape(REQUESTS, REQ_TOK, D)

    def one_request(item):
        block, ident = item
        down_rows = adapter_down[ident]
        up_rows = adapter_up[ident]
        shrunk = lax.dot_general(block, down_rows, (((1,), (1,)), ((), ())), preferred_element_type=jnp.float32).astype(jnp.bfloat16)
        return jnp.dot(shrunk, up_rows, preferred_element_type=jnp.float32).astype(jnp.bfloat16)

    deltas = lax.map(one_request, (blocks, req_adapter.astype(jnp.int32)))
    total = base + deltas.reshape(TOKENS, KVW).astype(jnp.float32)
    return total.astype(jnp.bfloat16)
```

```python
import jax
import jax.numpy as jnp
from jax import lax
from jax.experimental import pallas as pl
from jax.experimental.pallas import tpu as pltpu
from jax.sharding import PartitionSpec as P

MESH = pl.DeviceIdType.MESH
PLANES = 4
CHUNKS = 2
TILE = 256


def gathered(tokens, req_adapter, value_weight, adapter_down, adapter_up):
    partial_base = jnp.dot(tokens, value_weight, preferred_element_type=jnp.float32)
    base = lax.psum_scatter(partial_base, "narrow", scatter_dimension=1, tiled=True)
    tok_count = tokens.shape[0]
    half_width = tokens.shape[1]
    req_count = req_adapter.shape[0]
    req_len = tok_count // req_count
    col_count = adapter_up.shape[2]
    blocks = tokens.reshape(req_count, req_len, half_width)
    chosen = jnp.take(lax.all_gather(adapter_down, "dp", axis=1, tiled=True), req_adapter, axis=0)
    result = jnp.einsum("qtd,qrd->qtr", blocks, chosen, preferred_element_type=jnp.float32)
    shrunk = lax.psum(result, "narrow").astype(jnp.bfloat16)
    chosen = jnp.take(lax.all_gather(adapter_up, "dp", axis=1, tiled=True), req_adapter, axis=0)
    delta = jnp.einsum("qtr,qrc->qtc", shrunk, chosen, preferred_element_type=jnp.float32)
    delta = delta.astype(jnp.bfloat16).reshape(tok_count, col_count)
    return (base + delta.astype(jnp.float32)).astype(jnp.bfloat16)


def kernel(
    req_ref, tok_hbm, w_hbm, down_hbm, up_hbm, out_ref,
    tok, w, slots, pack, recv, ids_v, ids_s, peer_base, got_base, own_base, part, got_part,
    load_sem, zload_sem, idload_sem, z_send, z_recv, p_send, p_recv, id_send, id_recv,
    base_send, base_recv, part_send, part_recv,
):
    g, d, c = lax.axis_index("groups"), lax.axis_index("dp"), lax.axis_index("narrow")
    z, y = d // 2, d % 2
    requests = recv.shape[1]
    rows = tok.shape[0] // requests
    rank = down_hbm.shape[1]
    dhalf = down_hbm.shape[2] // 2
    uhalf = up_hbm.shape[2] // 2
    wide = recv.shape[-1]

    def slot(way, step, chunk):
        return slots[chunk * (2 * PLANES - 1) + (0 if step < 0 else 1 + way * (PLANES - 1) + step)]

    cols = out_ref.shape[1]
    above, below = (g, d + 2, c), (g, d - 2, c)
    yflip = d + 1 - 2 * y
    around = ((1 - g, d, c), (g, yflip, c), (1 - g, yflip, c))
    other = (g, d, 1 - c)

    zloads = []
    for chunk in range(CHUNKS):
        low, high = chunk * wide, (chunk + 1) * wide
        pieces = []
        if low < dhalf:
            size = min(high, dhalf) - low
            src = pl.ds(pl.multiple_of(g * dhalf + low, 128), size)
            pieces.append((down_hbm.at[:, :, src], slot(0, -1, chunk).at[:, :, pl.ds(0, size)]))
        if high > dhalf:
            start = max(low, dhalf)
            size = high - start
            src = pl.ds(pl.multiple_of(g * uhalf + start - dhalf, 128), size)
            pieces.append((up_hbm.at[:, :, src], slot(0, -1, chunk).at[:, :, pl.ds(start - low, size)]))
        for place, (src, dst) in enumerate(pieces):
            copy = pltpu.make_async_copy(src, dst, zload_sem.at[chunk, place])
            copy.start()
            zloads.append((chunk, copy))
    tok_load = pltpu.make_async_copy(tok_hbm, tok, load_sem.at[0])
    w_load = pltpu.make_async_copy(w_hbm, w, load_sem.at[1])
    tok_load.start()
    w_load.start()

    lane = lax.broadcasted_iota(jnp.int32, ids_v.shape[1:], 1)
    ids = jnp.zeros(ids_v.shape[1:], jnp.int32)
    for q in range(requests):
        ids = jnp.where(lane == q, req_ref[q], ids)
    ids_v[3] = ids

    barrier = pltpu.get_barrier_semaphore()
    for target in around + (other,):
        pl.semaphore_signal(barrier, inc=1, device_id=target, device_id_type=MESH)

    @pl.when(z < PLANES - 1)
    def _():
        pl.semaphore_signal(barrier, inc=1, device_id=above, device_id_type=MESH)

    @pl.when(z > 0)
    def _():
        pl.semaphore_signal(barrier, inc=1, device_id=below, device_id_type=MESH)

    pl.semaphore_wait(barrier, 4 + (z + PLANES - 1) // PLANES + (2 * PLANES - 2 - z) // PLANES)

    def z_copy(way, step, chunk):
        return pltpu.make_async_remote_copy(
            src_ref=slot(way, step - 1, chunk), dst_ref=slot(way, step, chunk),
            send_sem=z_send.at[way, step, chunk], recv_sem=z_recv.at[way, step, chunk],
            device_id=above if way == 0 else below, device_id_type=MESH,
        )

    def z_sends(way, step):
        return z - step >= 0 if way == 0 else z + step <= PLANES - 1

    def z_can(way, step):
        if way == 0:
            return jnp.logical_and(z < PLANES - 1, z_sends(way, step))
        return jnp.logical_and(z > 0, z_sends(way, step))

    def z_arrives(way, step):
        return z - 1 - step >= 0 if way == 0 else z + 1 + step <= PLANES - 1

    def p_copy(block, relation, chunk):
        return pltpu.make_async_remote_copy(
            src_ref=pack.at[chunk, block, relation],
            dst_ref=recv.at[chunk, :, g, block, y],
            send_sem=p_send.at[chunk, block, relation], recv_sem=p_recv.at[chunk, block, relation],
            device_id=around[relation], device_id_type=MESH,
        )

    def p_arrival(block, relation, chunk):
        from_g = g if relation == 1 else 1 - g
        from_y = y if relation == 0 else 1 - y
        return pltpu.make_async_remote_copy(
            src_ref=pack.at[chunk, block, relation],
            dst_ref=recv.at[chunk, :, from_g, block, from_y],
            send_sem=p_send.at[chunk, block, relation], recv_sem=p_recv.at[chunk, block, relation],
            device_id=around[relation], device_id_type=MESH,
        )

    def share(way, step, chunk):
        held = slot(way, step, chunk)
        block = z - 1 - step if way == 0 else z + 1 + step
        for relation in (2, 0, 1):
            for q in range(requests):
                pack[chunk, block, relation, q] = held[ids_s[relation, 0, q]]
            p_copy(block, relation, chunk).start()
        for q in range(requests):
            recv[chunk, q, g, block, y] = held[req_ref[q]]

    def id_copy(relation):
        return pltpu.make_async_remote_copy(
            src_ref=ids_v.at[3], dst_ref=ids_v.at[relation],
            send_sem=id_send.at[relation], recv_sem=id_recv.at[relation],
            device_id=around[relation], device_id_type=MESH,
        )

    for relation in range(3):
        id_copy(relation).start()
    for chunk in range(CHUNKS):
        for which, copy in zloads:
            if which == chunk:
                copy.wait()
        for way in range(2):
            @pl.when(z_can(way, 0))
            def _():
                z_copy(way, 0, chunk).start()

    for relation in range(3):
        id_copy(relation).wait()
        id_load = pltpu.make_async_copy(ids_v.at[relation], ids_s.at[relation], idload_sem.at[relation])
        id_load.start()
        id_load.wait()
    for chunk in range(CHUNKS):
        share(0, -1, chunk)

    tok_load.wait()
    w_load.wait()

    m_tiles = tok.shape[0] // TILE
    n_tiles = cols // TILE

    def base(first, dst, low, high):
        def tile(i, _):
            n, m = i // m_tiles, i % m_tiles
            at = pl.ds(pl.multiple_of(m * TILE, TILE), TILE)
            dst[at, pl.ds(pl.multiple_of(n * TILE, TILE), TILE)] = jnp.dot(
                tok[at, :], w[:, pl.ds(pl.multiple_of(first + n * TILE, TILE), TILE)],
                preferred_element_type=jnp.float32,
            )
            return 0

        lax.fori_loop(low, high, tile, 0)

    base_copy = pltpu.make_async_remote_copy(
        src_ref=peer_base, dst_ref=got_base, send_sem=base_send, recv_sem=base_recv,
        device_id=other, device_id_type=MESH,
    )
    tiles = m_tiles * n_tiles

    def pass_on(step, chunk):
        for way in range(2):
            @pl.when(z_arrives(way, step))
            def _():
                z_copy(way, step, chunk).wait_recv()
        if step + 1 < PLANES - 1:
            for way in range(2):
                @pl.when(z_can(way, step + 1))
                def _():
                    z_copy(way, step + 1, chunk).start()
        for way in range(2):
            @pl.when(z_arrives(way, step))
            def _():
                share(way, step, chunk)

    base((1 - c) * cols, peer_base, 0, tiles)
    base_copy.start()
    pass_on(0, 0)
    base(c * cols, own_base, 0, tiles // 2)
    pass_on(0, 1)
    base(c * cols, own_base, tiles // 2, tiles)
    for step in range(1, PLANES - 1):
        for chunk in range(CHUNKS):
            pass_on(step, chunk)

    for chunk in range(CHUNKS):
        for block in range(PLANES):
            for relation in range(3):
                p_arrival(block, relation, chunk).wait_recv()

    full = PLANES * 2 * rank

    def picked(q, side, chunk):
        rows8 = recv[chunk, q, side].astype(jnp.float32)
        return rows8.reshape(full, wide).astype(jnp.bfloat16)

    def part_copy(q):
        return pltpu.make_async_remote_copy(
            src_ref=part.at[q], dst_ref=got_part.at[q],
            send_sem=part_send.at[q], recv_sem=part_recv.at[q],
            device_id=other, device_id_type=MESH,
        )

    for q in range(requests):
        at = pl.ds(q * rows, rows)
        total = jnp.zeros((rows, full), jnp.float32)
        for side in range(2):
            for chunk in range(CHUNKS):
                low = chunk * wide
                size = min(low + wide, dhalf) - low
                if size > 0:
                    total += lax.dot_general(
                        tok[at, pl.ds(side * dhalf + low, size)], picked(q, side, chunk)[:, :size],
                        (((1,), (1,)), ((), ())), preferred_element_type=jnp.float32,
                    )
        part[q] = total
        part_copy(q).start()

    base_copy.wait()
    for q in range(requests):
        at = pl.ds(q * rows, rows)
        part_copy(q).wait()
        shrunk = (part[q] + got_part[q]).astype(jnp.bfloat16)
        for side in range(2):
            to = pl.ds(side * uhalf, uhalf)
            up = picked(q, side, CHUNKS - 1)[:, wide - uhalf:]
            delta = jnp.dot(shrunk, up, preferred_element_type=jnp.float32).astype(jnp.bfloat16)
            total = own_base[at, to] + got_base[at, to] + delta.astype(jnp.float32)
            out_ref[at, to] = total.astype(jnp.bfloat16)

    for chunk in range(CHUNKS):
        for step in range(PLANES - 1):
            for way in range(2):
                @pl.when(z_can(way, step))
                def _():
                    z_copy(way, step, chunk).wait_send()
        for block in range(PLANES):
            for relation in range(3):
                p_copy(block, relation, chunk).wait_send()


def fused(tokens, req_adapter, value_weight, adapter_down, adapter_up):
    tok_count, width = tokens.shape
    requests = req_adapter.shape[0]
    adapters, rank, _ = adapter_down.shape
    cols = adapter_up.shape[2]
    wide = (width + cols) // 2 // CHUNKS
    rows = tok_count // requests
    full = PLANES * 2 * rank
    anywhere = pl.BlockSpec(memory_space=pl.ANY)
    dma = pltpu.SemaphoreType.DMA
    return pl.pallas_call(
        kernel,
        out_shape=jax.ShapeDtypeStruct((tok_count, cols), jnp.bfloat16),
        in_specs=[pl.BlockSpec(memory_space=pltpu.SMEM)] + [anywhere] * 4,
        out_specs=pl.BlockSpec(memory_space=pltpu.VMEM),
        scratch_shapes=[
            pltpu.VMEM(tokens.shape, jnp.bfloat16),
            pltpu.VMEM(value_weight.shape, jnp.bfloat16),
            [pltpu.VMEM((adapters, rank, wide), jnp.bfloat16)] * (CHUNKS * (2 * PLANES - 1)),
            pltpu.VMEM((CHUNKS, PLANES, 3, requests, rank, wide), jnp.bfloat16),
            pltpu.VMEM((CHUNKS, requests, 2, PLANES, 2, rank, wide), jnp.bfloat16),
            pltpu.VMEM((4, 8, 128), jnp.int32),
            pltpu.SMEM((3, 8, 128), jnp.int32),
            pltpu.VMEM((tok_count, cols), jnp.float32),
            pltpu.VMEM((tok_count, cols), jnp.float32),
            pltpu.VMEM((tok_count, cols), jnp.float32),
            pltpu.VMEM((requests, rows, full), jnp.float32),
            pltpu.VMEM((requests, rows, full), jnp.float32),
            dma((2,)),
            dma((CHUNKS, 2)),
            dma((3,)),
            dma((2, PLANES - 1, CHUNKS)),
            dma((2, PLANES - 1, CHUNKS)),
            dma((CHUNKS, PLANES, 3)),
            dma((CHUNKS, PLANES, 3)),
            dma((3,)),
            dma((3,)),
            dma,
            dma,
            dma((requests,)),
            dma((requests,)),
        ],
        compiler_params=pltpu.CompilerParams(
            collective_id=0, has_side_effects=True, vmem_limit_bytes=56 * 2**20
        ),
        cost_estimate=pl.CostEstimate(
            flops=2 * tok_count * width * (2 * cols + full),
            bytes_accessed=2 * (tok_count * width + width * 2 * cols),
            transcendentals=0,
        ),
    )(req_adapter, tokens, value_weight, adapter_down, adapter_up)


def solution(mesh):
    in_specs = (
        P(("groups", "dp"), "narrow"),
        P(("groups", "dp")),
        P("narrow", None),
        P(None, "dp", "narrow"),
        P(None, "dp", "narrow"),
    )
    out_specs = P(("groups", "dp"), "narrow")
    small = mesh.shape["groups"] == 2 and mesh.shape["dp"] == 2 * PLANES
    return jax.shard_map(
        fused if small else gathered,
        mesh=mesh, in_specs=in_specs, out_specs=out_specs, check_vma=False,
    )
```

```python
import jax
import jax.numpy as jnp
from jax import lax
from jax.experimental import pallas as pl
from jax.experimental.pallas import tpu as pltpu
from jax.sharding import PartitionSpec as P

MESH = pl.DeviceIdType.MESH
PLANES = 4
CHUNKS = 3
TILE = 256


def gathered(tokens, req_adapter, value_weight, adapter_down, adapter_up):
    partial_base = jnp.dot(tokens, value_weight, preferred_element_type=jnp.float32)
    base = lax.psum_scatter(partial_base, "narrow", scatter_dimension=1, tiled=True)
    tok_count = tokens.shape[0]
    half_width = tokens.shape[1]
    req_count = req_adapter.shape[0]
    req_len = tok_count // req_count
    col_count = adapter_up.shape[2]
    blocks = tokens.reshape(req_count, req_len, half_width)
    chosen = jnp.take(lax.all_gather(adapter_down, "dp", axis=1, tiled=True), req_adapter, axis=0)
    result = jnp.einsum("qtd,qrd->qtr", blocks, chosen, preferred_element_type=jnp.float32)
    shrunk = lax.psum(result, "narrow").astype(jnp.bfloat16)
    chosen = jnp.take(lax.all_gather(adapter_up, "dp", axis=1, tiled=True), req_adapter, axis=0)
    delta = jnp.einsum("qtr,qrc->qtc", shrunk, chosen, preferred_element_type=jnp.float32)
    delta = delta.astype(jnp.bfloat16).reshape(tok_count, col_count)
    return (base + delta.astype(jnp.float32)).astype(jnp.bfloat16)


def kernel(
    req_ref, tok_hbm, w_hbm, down_hbm, up_hbm, out_ref,
    tok, w, slots, pack, recv, ids_v, ids_s, peer_base, got_base, own_base, part, got_part,
    load_sem, zload_sem, idload_sem, z_send, z_recv, p_send, p_recv, id_send, id_recv,
    base_send, base_recv, part_send, part_recv,
):
    g, d, c = lax.axis_index("groups"), lax.axis_index("dp"), lax.axis_index("narrow")
    z, y = d // 2, d % 2
    requests = recv.shape[1]
    rows = tok.shape[0] // requests
    rank = down_hbm.shape[1]
    dhalf = down_hbm.shape[2] // 2
    uhalf = up_hbm.shape[2] // 2
    wide = recv.shape[-1]

    def slot(way, step, chunk):
        return slots[chunk * (2 * PLANES - 1) + (0 if step < 0 else 1 + way * (PLANES - 1) + step)]

    cols = out_ref.shape[1]
    above, below = (g, d + 2, c), (g, d - 2, c)
    yflip = d + 1 - 2 * y
    around = ((1 - g, d, c), (g, yflip, c), (1 - g, yflip, c))
    other = (g, d, 1 - c)

    barrier = pltpu.get_barrier_semaphore()
    for target in around + (other,):
        pl.semaphore_signal(barrier, inc=1, device_id=target, device_id_type=MESH)

    @pl.when(z < PLANES - 1)
    def _():
        pl.semaphore_signal(barrier, inc=1, device_id=above, device_id_type=MESH)

    @pl.when(z > 0)
    def _():
        pl.semaphore_signal(barrier, inc=1, device_id=below, device_id_type=MESH)

    zloads = []
    for chunk in range(CHUNKS):
        low, high = chunk * wide, (chunk + 1) * wide
        pieces = []
        if low < dhalf:
            size = min(high, dhalf) - low
            src = pl.ds(pl.multiple_of(g * dhalf + low, 128), size)
            pieces.append((down_hbm.at[:, :, src], slot(0, -1, chunk).at[:, :, pl.ds(0, size)]))
        if high > dhalf:
            start = max(low, dhalf)
            size = high - start
            src = pl.ds(pl.multiple_of(g * uhalf + start - dhalf, 128), size)
            pieces.append((up_hbm.at[:, :, src], slot(0, -1, chunk).at[:, :, pl.ds(start - low, size)]))
        for place, (src, dst) in enumerate(pieces):
            copy = pltpu.make_async_copy(src, dst, zload_sem.at[chunk, place])
            copy.start()
            zloads.append((chunk, copy))
    tok_load = pltpu.make_async_copy(tok_hbm, tok, load_sem.at[0])
    w_load = pltpu.make_async_copy(w_hbm, w, load_sem.at[1])

    lane = lax.broadcasted_iota(jnp.int32, ids_v.shape[1:], 1)
    ids = jnp.zeros(ids_v.shape[1:], jnp.int32)
    for q in range(requests):
        ids = jnp.where(lane == q, req_ref[q], ids)
    ids_v[3] = ids

    pl.semaphore_wait(barrier, 4 + (z + PLANES - 1) // PLANES + (2 * PLANES - 2 - z) // PLANES)

    def z_copy(way, step, chunk):
        return pltpu.make_async_remote_copy(
            src_ref=slot(way, step - 1, chunk), dst_ref=slot(way, step, chunk),
            send_sem=z_send.at[way, step, chunk], recv_sem=z_recv.at[way, step, chunk],
            device_id=above if way == 0 else below, device_id_type=MESH,
        )

    def z_sends(way, step):
        return z - step >= 0 if way == 0 else z + step <= PLANES - 1

    def z_can(way, step):
        if way == 0:
            return jnp.logical_and(z < PLANES - 1, z_sends(way, step))
        return jnp.logical_and(z > 0, z_sends(way, step))

    def z_arrives(way, step):
        return z - 1 - step >= 0 if way == 0 else z + 1 + step <= PLANES - 1

    def p_copy(block, relation, chunk):
        return pltpu.make_async_remote_copy(
            src_ref=pack.at[chunk, block, relation],
            dst_ref=recv.at[chunk, :, g, block, y],
            send_sem=p_send.at[chunk, block, relation], recv_sem=p_recv.at[chunk, block, relation],
            device_id=around[relation], device_id_type=MESH,
        )

    def p_arrival(block, relation, chunk):
        from_g = g if relation == 1 else 1 - g
        from_y = y if relation == 0 else 1 - y
        return pltpu.make_async_remote_copy(
            src_ref=pack.at[chunk, block, relation],
            dst_ref=recv.at[chunk, :, from_g, block, from_y],
            send_sem=p_send.at[chunk, block, relation], recv_sem=p_recv.at[chunk, block, relation],
            device_id=around[relation], device_id_type=MESH,
        )

    def share(way, step, chunk):
        held = slot(way, step, chunk)
        block = z - 1 - step if way == 0 else z + 1 + step
        for relation in (2, 0, 1):
            for q in range(requests):
                pack[chunk, block, relation, q] = held[ids_s[relation, 0, q]]
            p_copy(block, relation, chunk).start()
        for q in range(requests):
            recv[chunk, q, g, block, y] = held[req_ref[q]]

    def id_copy(relation):
        return pltpu.make_async_remote_copy(
            src_ref=ids_v.at[3], dst_ref=ids_v.at[relation],
            send_sem=id_send.at[relation], recv_sem=id_recv.at[relation],
            device_id=around[relation], device_id_type=MESH,
        )

    for chunk in range(CHUNKS):
        for which, copy in zloads:
            if which == chunk:
                copy.wait()
        for way in range(2):
            @pl.when(z_can(way, 0))
            def _():
                z_copy(way, 0, chunk).start()

        if chunk == 0:
            for relation in range(3):
                id_copy(relation).start()
    tok_load.start()
    w_load.start()

    for relation in range(3):
        id_copy(relation).wait()
        id_load = pltpu.make_async_copy(ids_v.at[relation], ids_s.at[relation], idload_sem.at[relation])
        id_load.start()
        id_load.wait()
    for chunk in range(CHUNKS):
        share(0, -1, chunk)

    tok_load.wait()
    w_load.wait()

    m_tiles = tok.shape[0] // TILE
    n_tiles = cols // TILE

    def base(first, dst, low, high):
        def tile(i, _):
            n, m = i // m_tiles, i % m_tiles
            at = pl.ds(pl.multiple_of(m * TILE, TILE), TILE)
            dst[at, pl.ds(pl.multiple_of(n * TILE, TILE), TILE)] = jnp.dot(
                tok[at, :], w[:, pl.ds(pl.multiple_of(first + n * TILE, TILE), TILE)],
                preferred_element_type=jnp.float32,
            )
            return 0

        lax.fori_loop(low, high, tile, 0)

    base_copy = pltpu.make_async_remote_copy(
        src_ref=peer_base, dst_ref=got_base, send_sem=base_send, recv_sem=base_recv,
        device_id=other, device_id_type=MESH,
    )
    tiles = m_tiles * n_tiles

    def pass_on(step, chunk):
        for way in range(2):
            @pl.when(z_arrives(way, step))
            def _():
                z_copy(way, step, chunk).wait_recv()
        if step + 1 < PLANES - 1:
            for way in range(2):
                @pl.when(z_can(way, step + 1))
                def _():
                    z_copy(way, step + 1, chunk).start()
        for way in range(2):
            @pl.when(z_arrives(way, step))
            def _():
                share(way, step, chunk)

    base((1 - c) * cols, peer_base, 0, tiles // 2)
    pass_on(0, 0)
    base((1 - c) * cols, peer_base, tiles // 2, tiles)
    base_copy.start()
    pass_on(0, 1)
    base(c * cols, own_base, 0, tiles // 2)
    for chunk in range(2, CHUNKS):
        pass_on(0, chunk)
    base(c * cols, own_base, tiles // 2, tiles)
    for chunk in range(CHUNKS):
        pass_on(1, chunk)

    full = PLANES * 2 * rank

    def picked(q, side, chunk):
        rows8 = recv[chunk, q, side].astype(jnp.float32)
        return rows8.reshape(full, wide).astype(jnp.bfloat16)

    def part_copy(q):
        return pltpu.make_async_remote_copy(
            src_ref=part.at[q], dst_ref=got_part.at[q],
            send_sem=part_send.at[q], recv_sem=part_recv.at[q],
            device_id=other, device_id_type=MESH,
        )

    def shrink(chunk):
        for block in range(PLANES):
            for relation in range(3):
                p_arrival(block, relation, chunk).wait_recv()
        low = chunk * wide
        size = min(low + wide, dhalf) - low
        for q in range(requests):
            at = pl.ds(q * rows, rows)
            total = jnp.zeros((rows, full), jnp.float32) if chunk == 0 else part[q]
            for side in range(2):
                total += lax.dot_general(
                    tok[at, pl.ds(side * dhalf + low, size)], picked(q, side, chunk)[:, :size],
                    (((1,), (1,)), ((), ())), preferred_element_type=jnp.float32,
                )
            part[q] = total
            if chunk == CHUNKS - 1:
                part_copy(q).start()

    for chunk in range(CHUNKS):
        pass_on(2, chunk)
        if chunk > 0:
            shrink(chunk - 1)
    shrink(CHUNKS - 1)

    base_copy.wait()
    for q in range(requests):
        at = pl.ds(q * rows, rows)
        part_copy(q).wait()
        shrunk = (part[q] + got_part[q]).astype(jnp.bfloat16)
        for side in range(2):
            to = pl.ds(side * uhalf, uhalf)
            up = picked(q, side, CHUNKS - 1)[:, wide - uhalf:]
            delta = jnp.dot(shrunk, up, preferred_element_type=jnp.float32).astype(jnp.bfloat16)
            total = own_base[at, to] + got_base[at, to] + delta.astype(jnp.float32)
            out_ref[at, to] = total.astype(jnp.bfloat16)

    for chunk in range(CHUNKS):
        for step in range(PLANES - 1):
            for way in range(2):
                @pl.when(z_can(way, step))
                def _():
                    z_copy(way, step, chunk).wait_send()
        for block in range(PLANES):
            for relation in range(3):
                p_copy(block, relation, chunk).wait_send()


def fused(tokens, req_adapter, value_weight, adapter_down, adapter_up):
    tok_count, width = tokens.shape
    requests = req_adapter.shape[0]
    adapters, rank, _ = adapter_down.shape
    cols = adapter_up.shape[2]
    wide = (width + cols) // 2 // CHUNKS
    rows = tok_count // requests
    full = PLANES * 2 * rank
    anywhere = pl.BlockSpec(memory_space=pl.ANY)
    dma = pltpu.SemaphoreType.DMA
    return pl.pallas_call(
        kernel,
        out_shape=jax.ShapeDtypeStruct((tok_count, cols), jnp.bfloat16),
        in_specs=[pl.BlockSpec(memory_space=pltpu.SMEM)] + [anywhere] * 4,
        out_specs=pl.BlockSpec(memory_space=pltpu.VMEM),
        scratch_shapes=[
            pltpu.VMEM(tokens.shape, jnp.bfloat16),
            pltpu.VMEM(value_weight.shape, jnp.bfloat16),
            [pltpu.VMEM((adapters, rank, wide), jnp.bfloat16)] * (CHUNKS * (2 * PLANES - 1)),
            pltpu.VMEM((CHUNKS, PLANES, 3, requests, rank, wide), jnp.bfloat16),
            pltpu.VMEM((CHUNKS, requests, 2, PLANES, 2, rank, wide), jnp.bfloat16),
            pltpu.VMEM((4, 8, 128), jnp.int32),
            pltpu.SMEM((3, 8, 128), jnp.int32),
            pltpu.VMEM((tok_count, cols), jnp.float32),
            pltpu.VMEM((tok_count, cols), jnp.float32),
            pltpu.VMEM((tok_count, cols), jnp.float32),
            pltpu.VMEM((requests, rows, full), jnp.float32),
            pltpu.VMEM((requests, rows, full), jnp.float32),
            dma((2,)),
            dma((CHUNKS, 2)),
            dma((3,)),
            dma((2, PLANES - 1, CHUNKS)),
            dma((2, PLANES - 1, CHUNKS)),
            dma((CHUNKS, PLANES, 3)),
            dma((CHUNKS, PLANES, 3)),
            dma((3,)),
            dma((3,)),
            dma,
            dma,
            dma((requests,)),
            dma((requests,)),
        ],
        compiler_params=pltpu.CompilerParams(
            collective_id=0, has_side_effects=True, vmem_limit_bytes=56 * 2**20
        ),
        cost_estimate=pl.CostEstimate(
            flops=2 * tok_count * width * (2 * cols + full),
            bytes_accessed=2 * (tok_count * width + width * 2 * cols),
            transcendentals=0,
        ),
    )(req_adapter, tokens, value_weight, adapter_down, adapter_up)


def solution(mesh):
    in_specs = (
        P(("groups", "dp"), "narrow"),
        P(("groups", "dp")),
        P("narrow", None),
        P(None, "dp", "narrow"),
        P(None, "dp", "narrow"),
    )
    out_specs = P(("groups", "dp"), "narrow")
    small = mesh.shape["groups"] == 2 and mesh.shape["dp"] == 2 * PLANES
    return jax.shard_map(
        fused if small else gathered,
        mesh=mesh, in_specs=in_specs, out_specs=out_specs, check_vma=False,
    )
```

```python
import jax
import jax.numpy as jnp
from jax import lax
from jax.experimental import pallas as pl
from jax.experimental.pallas import tpu as pltpu
from jax.sharding import PartitionSpec as P

MESH = pl.DeviceIdType.MESH
PLANES = 4
CHUNKS = 3
TILE = 256


def gathered(tokens, req_adapter, value_weight, adapter_down, adapter_up):
    partial_base = jnp.dot(tokens, value_weight, preferred_element_type=jnp.float32)
    base = lax.psum_scatter(partial_base, "narrow", scatter_dimension=1, tiled=True)
    tok_count = tokens.shape[0]
    half_width = tokens.shape[1]
    req_count = req_adapter.shape[0]
    req_len = tok_count // req_count
    col_count = adapter_up.shape[2]
    blocks = tokens.reshape(req_count, req_len, half_width)
    chosen = jnp.take(lax.all_gather(adapter_down, "dp", axis=1, tiled=True), req_adapter, axis=0)
    result = jnp.einsum("qtd,qrd->qtr", blocks, chosen, preferred_element_type=jnp.float32)
    shrunk = lax.psum(result, "narrow").astype(jnp.bfloat16)
    chosen = jnp.take(lax.all_gather(adapter_up, "dp", axis=1, tiled=True), req_adapter, axis=0)
    delta = jnp.einsum("qtr,qrc->qtc", shrunk, chosen, preferred_element_type=jnp.float32)
    delta = delta.astype(jnp.bfloat16).reshape(tok_count, col_count)
    return (base + delta.astype(jnp.float32)).astype(jnp.bfloat16)


def kernel(
    req_ref, tok_hbm, w_hbm, down_hbm, up_hbm, out_ref,
    tok, w, slots, pack, recv, ids_v, ids_s, peer_base, got_base, own_base, part, got_part,
    load_sem, zload_sem, idload_sem, z_send, z_recv, p_send, p_recv, id_send, id_recv,
    base_send, base_recv, part_send, part_recv,
):
    g, d, c = lax.axis_index("groups"), lax.axis_index("dp"), lax.axis_index("narrow")
    z, y = d // 2, d % 2
    requests = recv.shape[1]
    rows = tok.shape[0] // requests
    rank = down_hbm.shape[1]
    dhalf = down_hbm.shape[2] // 2
    uhalf = up_hbm.shape[2] // 2
    wide = recv.shape[-1]

    def slot(way, step, chunk):
        return slots[chunk * (2 * PLANES - 1) + (0 if step < 0 else 1 + way * (PLANES - 1) + step)]

    cols = out_ref.shape[1]
    above, below = (g, d + 2, c), (g, d - 2, c)
    yflip = d + 1 - 2 * y
    around = ((1 - g, d, c), (g, yflip, c), (1 - g, yflip, c))
    other = (g, d, 1 - c)

    barrier = pltpu.get_barrier_semaphore()
    for target in around + (other,):
        pl.semaphore_signal(barrier, inc=1, device_id=target, device_id_type=MESH)

    @pl.when(z < PLANES - 1)
    def _():
        pl.semaphore_signal(barrier, inc=1, device_id=above, device_id_type=MESH)

    @pl.when(z > 0)
    def _():
        pl.semaphore_signal(barrier, inc=1, device_id=below, device_id_type=MESH)

    zloads = []
    for chunk in range(CHUNKS):
        low, high = chunk * wide, (chunk + 1) * wide
        pieces = []
        if low < dhalf:
            size = min(high, dhalf) - low
            src = pl.ds(pl.multiple_of(g * dhalf + low, 128), size)
            pieces.append((down_hbm.at[:, :, src], slot(0, -1, chunk).at[:, :, pl.ds(0, size)]))
        if high > dhalf:
            start = max(low, dhalf)
            size = high - start
            src = pl.ds(pl.multiple_of(g * uhalf + start - dhalf, 128), size)
            pieces.append((up_hbm.at[:, :, src], slot(0, -1, chunk).at[:, :, pl.ds(start - low, size)]))
        for place, (src, dst) in enumerate(pieces):
            copy = pltpu.make_async_copy(src, dst, zload_sem.at[chunk, place])
            copy.start()
            zloads.append((chunk, copy))
    tok_load = pltpu.make_async_copy(tok_hbm, tok, load_sem.at[0])
    w_load = pltpu.make_async_copy(w_hbm, w, load_sem.at[1])

    lane = lax.broadcasted_iota(jnp.int32, ids_v.shape[1:], 1)
    ids = jnp.zeros(ids_v.shape[1:], jnp.int32)
    for q in range(requests):
        ids = jnp.where(lane == q, req_ref[q], ids)
    ids_v[3] = ids

    pl.semaphore_wait(barrier, 4 + (z + PLANES - 1) // PLANES + (2 * PLANES - 2 - z) // PLANES)

    def z_copy(way, step, chunk):
        return pltpu.make_async_remote_copy(
            src_ref=slot(way, step - 1, chunk), dst_ref=slot(way, step, chunk),
            send_sem=z_send.at[way, step, chunk], recv_sem=z_recv.at[way, step, chunk],
            device_id=above if way == 0 else below, device_id_type=MESH,
        )

    def z_sends(way, step):
        return z - step >= 0 if way == 0 else z + step <= PLANES - 1

    def z_can(way, step):
        if way == 0:
            return jnp.logical_and(z < PLANES - 1, z_sends(way, step))
        return jnp.logical_and(z > 0, z_sends(way, step))

    def z_arrives(way, step):
        return z - 1 - step >= 0 if way == 0 else z + 1 + step <= PLANES - 1

    def p_copy(block, relation, chunk):
        return pltpu.make_async_remote_copy(
            src_ref=pack.at[chunk, block, relation],
            dst_ref=recv.at[chunk, :, g, block, y],
            send_sem=p_send.at[chunk, block, relation], recv_sem=p_recv.at[chunk, block, relation],
            device_id=around[relation], device_id_type=MESH,
        )

    def p_arrival(block, relation, chunk):
        from_g = g if relation == 1 else 1 - g
        from_y = y if relation == 0 else 1 - y
        return pltpu.make_async_remote_copy(
            src_ref=pack.at[chunk, block, relation],
            dst_ref=recv.at[chunk, :, from_g, block, from_y],
            send_sem=p_send.at[chunk, block, relation], recv_sem=p_recv.at[chunk, block, relation],
            device_id=around[relation], device_id_type=MESH,
        )

    def share(way, step, chunk):
        held = slot(way, step, chunk)
        block = z - 1 - step if way == 0 else z + 1 + step
        for relation in (2, 0, 1):
            for q in range(requests):
                pack[chunk, block, relation, q] = held[ids_s[relation, 0, q]]
            p_copy(block, relation, chunk).start()
        for q in range(requests):
            recv[chunk, q, g, block, y] = held[req_ref[q]]

    def id_copy(relation):
        return pltpu.make_async_remote_copy(
            src_ref=ids_v.at[3], dst_ref=ids_v.at[relation],
            send_sem=id_send.at[relation], recv_sem=id_recv.at[relation],
            device_id=around[relation], device_id_type=MESH,
        )

    for chunk in range(CHUNKS):
        for which, copy in zloads:
            if which == chunk:
                copy.wait()
        for way in range(2):
            @pl.when(z_can(way, 0))
            def _():
                z_copy(way, 0, chunk).start()

        if chunk == 0:
            for relation in range(3):
                id_copy(relation).start()
    tok_load.start()
    w_load.start()

    for relation in range(3):
        id_copy(relation).wait()
    id_load = pltpu.make_async_copy(ids_v.at[pl.ds(0, 3)], ids_s, idload_sem.at[0])
    id_load.start()
    id_load.wait()
    for chunk in range(CHUNKS):
        share(0, -1, chunk)

    tok_load.wait()
    w_load.wait()

    m_tiles = tok.shape[0] // TILE
    n_tiles = cols // TILE

    def base(first, dst, low, high):
        def tile(i, _):
            n, m = i // m_tiles, i % m_tiles
            at = pl.ds(pl.multiple_of(m * TILE, TILE), TILE)
            dst[at, pl.ds(pl.multiple_of(n * TILE, TILE), TILE)] = jnp.dot(
                tok[at, :], w[:, pl.ds(pl.multiple_of(first + n * TILE, TILE), TILE)],
                preferred_element_type=jnp.float32,
            )
            return 0

        lax.fori_loop(low, high, tile, 0)

    base_copy = pltpu.make_async_remote_copy(
        src_ref=peer_base, dst_ref=got_base, send_sem=base_send, recv_sem=base_recv,
        device_id=other, device_id_type=MESH,
    )
    tiles = m_tiles * n_tiles

    def pass_on(step, chunk):
        for way in range(2):
            @pl.when(z_arrives(way, step))
            def _():
                z_copy(way, step, chunk).wait_recv()
        if step + 1 < PLANES - 1:
            for way in range(2):
                @pl.when(z_can(way, step + 1))
                def _():
                    z_copy(way, step + 1, chunk).start()
        for way in range(2):
            @pl.when(z_arrives(way, step))
            def _():
                share(way, step, chunk)

    base((1 - c) * cols, peer_base, 0, tiles // 2)
    pass_on(0, 0)
    base((1 - c) * cols, peer_base, tiles // 2, tiles)
    base_copy.start()
    pass_on(0, 1)
    base(c * cols, own_base, 0, tiles // 2)
    for chunk in range(2, CHUNKS):
        pass_on(0, chunk)
    base(c * cols, own_base, tiles // 2, tiles)
    for chunk in range(CHUNKS):
        pass_on(1, chunk)

    full = PLANES * 2 * rank

    def picked(q, side, chunk):
        rows8 = recv[chunk, q, side].astype(jnp.float32)
        return rows8.reshape(full, wide).astype(jnp.bfloat16)

    def part_copy(q):
        return pltpu.make_async_remote_copy(
            src_ref=part.at[q], dst_ref=got_part.at[q],
            send_sem=part_send.at[q], recv_sem=part_recv.at[q],
            device_id=other, device_id_type=MESH,
        )

    def shrink(chunk):
        for block in range(PLANES):
            for relation in range(3):
                p_arrival(block, relation, chunk).wait_recv()
        low = chunk * wide
        size = min(low + wide, dhalf) - low
        for q in range(requests):
            at = pl.ds(q * rows, rows)
            total = jnp.zeros((rows, full), jnp.float32) if chunk == 0 else part[q]
            for side in range(2):
                total += lax.dot_general(
                    tok[at, pl.ds(side * dhalf + low, size)], picked(q, side, chunk)[:, :size],
                    (((1,), (1,)), ((), ())), preferred_element_type=jnp.float32,
                )
            part[q] = total
            if chunk == CHUNKS - 1:
                part_copy(q).start()

    for chunk in range(CHUNKS):
        pass_on(2, chunk)
        if chunk > 0:
            shrink(chunk - 1)
    shrink(CHUNKS - 1)

    base_copy.wait()
    for q in range(requests):
        at = pl.ds(q * rows, rows)
        part_copy(q).wait()
        shrunk = (part[q] + got_part[q]).astype(jnp.bfloat16)
        for side in range(2):
            to = pl.ds(side * uhalf, uhalf)
            up = picked(q, side, CHUNKS - 1)[:, wide - uhalf:]
            delta = jnp.dot(shrunk, up, preferred_element_type=jnp.float32).astype(jnp.bfloat16)
            total = own_base[at, to] + got_base[at, to] + delta.astype(jnp.float32)
            out_ref[at, to] = total.astype(jnp.bfloat16)

    for chunk in range(CHUNKS):
        for step in range(PLANES - 1):
            for way in range(2):
                @pl.when(z_can(way, step))
                def _():
                    z_copy(way, step, chunk).wait_send()
        for block in range(PLANES):
            for relation in range(3):
                p_copy(block, relation, chunk).wait_send()


def fused(tokens, req_adapter, value_weight, adapter_down, adapter_up):
    tok_count, width = tokens.shape
    requests = req_adapter.shape[0]
    adapters, rank, _ = adapter_down.shape
    cols = adapter_up.shape[2]
    wide = (width + cols) // 2 // CHUNKS
    rows = tok_count // requests
    full = PLANES * 2 * rank
    anywhere = pl.BlockSpec(memory_space=pl.ANY)
    dma = pltpu.SemaphoreType.DMA
    return pl.pallas_call(
        kernel,
        out_shape=jax.ShapeDtypeStruct((tok_count, cols), jnp.bfloat16),
        in_specs=[pl.BlockSpec(memory_space=pltpu.SMEM)] + [anywhere] * 4,
        out_specs=pl.BlockSpec(memory_space=pltpu.VMEM),
        scratch_shapes=[
            pltpu.VMEM(tokens.shape, jnp.bfloat16),
            pltpu.VMEM(value_weight.shape, jnp.bfloat16),
            [pltpu.VMEM((adapters, rank, wide), jnp.bfloat16)] * (CHUNKS * (2 * PLANES - 1)),
            pltpu.VMEM((CHUNKS, PLANES, 3, requests, rank, wide), jnp.bfloat16),
            pltpu.VMEM((CHUNKS, requests, 2, PLANES, 2, rank, wide), jnp.bfloat16),
            pltpu.VMEM((4, 8, 128), jnp.int32),
            pltpu.SMEM((3, 8, 128), jnp.int32),
            pltpu.VMEM((tok_count, cols), jnp.float32),
            pltpu.VMEM((tok_count, cols), jnp.float32),
            pltpu.VMEM((tok_count, cols), jnp.float32),
            pltpu.VMEM((requests, rows, full), jnp.float32),
            pltpu.VMEM((requests, rows, full), jnp.float32),
            dma((2,)),
            dma((CHUNKS, 2)),
            dma((3,)),
            dma((2, PLANES - 1, CHUNKS)),
            dma((2, PLANES - 1, CHUNKS)),
            dma((CHUNKS, PLANES, 3)),
            dma((CHUNKS, PLANES, 3)),
            dma((3,)),
            dma((3,)),
            dma,
            dma,
            dma((requests,)),
            dma((requests,)),
        ],
        compiler_params=pltpu.CompilerParams(
            collective_id=0, has_side_effects=True, vmem_limit_bytes=56 * 2**20
        ),
        cost_estimate=pl.CostEstimate(
            flops=2 * tok_count * width * (2 * cols + full),
            bytes_accessed=2 * (tok_count * width + width * 2 * cols),
            transcendentals=0,
        ),
    )(req_adapter, tokens, value_weight, adapter_down, adapter_up)


def solution(mesh):
    in_specs = (
        P(("groups", "dp"), "narrow"),
        P(("groups", "dp")),
        P("narrow", None),
        P(None, "dp", "narrow"),
        P(None, "dp", "narrow"),
    )
    out_specs = P(("groups", "dp"), "narrow")
    small = mesh.shape["groups"] == 2 and mesh.shape["dp"] == 2 * PLANES
    return jax.shard_map(
        fused if small else gathered,
        mesh=mesh, in_specs=in_specs, out_specs=out_specs, check_vma=False,
    )
```
